32 devices in a mesh: parts: 2 (over x), ctx: 16 (over z, y, core).
Axes of the slice: x: 2, y: 2, z: 4, core: 2. Of those that a mesh axis runs over, the one named last changes fastest.
Arguments:
- queries: bfloat16 [256, 8192], P(('parts', 'ctx')), parts along dimension 0, may hold values from -24 to 24
- steer_ids: int32 [256], P(('parts', 'ctx')), parts along dimension 0, may hold values from 0 to 15
- steer_table: bfloat16 [16, 8192], replicated, may hold values from -3 to 3
- kv: bfloat16 [2, 32768, 1024], P(None, ('parts', 'ctx')), parts along dimension 1, may hold values from -4 to 4
- blocks: int32 [4, 128], P('parts'), parts along dimension 0, may hold values from 0 to 255, as said below
- w_out: bfloat16 [8192, 8192], P('ctx'), may hold values from -0.0625 to 0.0625
Outputs:
- projected: bfloat16 [256, 8192], P(('parts', 'ctx')), parts along dimension 0
The draws below stay inside these ranges and needn't reach their ends.
There are 2 independent parts, one for each index of `parts`. The reference program is written for one: setup_inputs(seed, part) draws one part's arguments, and reference() takes and returns one part's arrays. A program takes and returns all parts, laid end to end along the dimension named above; an argument that names none is the same for every part. Nothing has to cross between parts.
Inputs may be any that keep to these rules, and one draw needn't show every extreme that they name: Each row lists 128 distinct key blocks and always includes block 0 and block 255.
All inputs are finite; a program needn't handle non-finite values.
Results may differ from the reference program's by a relative error of at most 0.0066.
Values may be sent and summed in bfloat16 or wider, within the bound.
A program may use at most 64 MiB of HBM per device.

```python
import jax
import jax.numpy as jnp
from jax import lax

HEADS = 64
KV_HEADS = 8
HEAD = 128
D = 8192
QUERIES = 128
CTX_DEV = 1024
BLOCK = 64
STEERS = 16
CONTEXT = 16384
BLOCKS_DEV = 16
KEY_BLOCKS = 256
QUERY_BLOCKS = 2
KEEP = 128
N_CTX = 16


def draw_queries(key, part):
    inner_key = jax.random.fold_in(key, 11)
    base_draw = jnp.clip(jax.random.normal(inner_key, (QUERIES, D), jnp.float32), -4.0, 4.0)
    shaped = base_draw.reshape(QUERIES, HEADS, HEAD)
    return shaped.reshape(QUERIES, D).astype(jnp.bfloat16)


def draw_kv(key, part):
    inner_key = jax.random.fold_in(key, 23)
    values_all = jnp.clip(jax.random.normal(inner_key, (2, CONTEXT, KV_HEADS * HEAD), jnp.float32), -4.0, 4.0)
    return values_all.astype(jnp.bfloat16)


def draw_blocks(key, part):
    random_part = jax.random.randint(jax.random.fold_in(key, 31), (QUERY_BLOCKS, KEY_BLOCKS), 0, 1024)
    hot_shards = jax.random.randint(jax.random.fold_in(key, 32), (KEY_BLOCKS // BLOCKS_DEV,), 0, 3) * 512
    hot_blocks = jnp.repeat(hot_shards, BLOCKS_DEV)
    forced = jnp.zeros((KEY_BLOCKS,), jnp.int32).at[0].set(4096).at[KEY_BLOCKS - 1].set(4096)
    ranked = (random_part + hot_blocks[None, :] + forced[None, :]) * KEY_BLOCKS + jnp.arange(KEY_BLOCKS, dtype=jnp.int32)[None, :]
    top_values, chosen = lax.top_k(ranked, KEEP)
    return chosen.astype(jnp.int32)


def touch_ends(values, key, least, largest):
    shape = values.shape
    index_at = [jax.random.randint(jax.random.fold_in(key, axis), (), 0, shape[axis]) for axis in range(len(shape))]
    values = values.at[tuple(index_at)].set(least)
    longest = shape.index(max(shape))
    index_at[longest] = (index_at[longest] + 1) % shape[longest]
    return values.at[tuple(index_at)].set(largest)


def shard_levels(stream_key, dims, shards, smallest, high):
    loudness = 1.0
    for axis_at, blocks in shards:
        draws = jax.random.uniform(jax.random.fold_in(jax.random.fold_in(stream_key, 6), axis_at), (blocks,), jnp.float32, smallest / len(shards), high / len(shards))
        loudness = loudness * jnp.repeat(jnp.exp(draws), dims[axis_at] // blocks).reshape((-1,) + (1,) * (len(dims) - 1 - axis_at))
    return loudness


def normal_values(rng, shape, deviation, most, shards=(), kind=jnp.bfloat16):
    entries = jax.random.normal(rng, shape, jnp.float32) * deviation
    if len(shards) > 0:
        entries = shard_levels(rng, shape, shards, -0.22, 0.18) * entries
    return jnp.clip(entries, min=-most, max=most).astype(kind)


def setup_inputs(seed: int = 0, part: int = 0) -> dict:
    streams_of = jax.random.split(jax.random.key(seed), 7)
    part_splits = jax.random.split(jax.random.fold_in(streams_of[6], part), 7)
    return {
        "queries": draw_queries(jax.random.fold_in(jax.random.fold_in(streams_of[6], part), 71), part),
        "steer_ids": touch_ends(jax.random.randint(part_splits[1], (QUERIES,), 0, STEERS), jax.random.fold_in(part_splits[1], 1), 0, STEERS - 1).astype(jnp.int32),
        "steer_table": normal_values(streams_of[2], (STEERS, D), 0.5, 3.0),
        "kv": draw_kv(jax.random.fold_in(jax.random.fold_in(streams_of[6], part), 71), part),
        "blocks": draw_blocks(jax.random.fold_in(jax.random.fold_in(streams_of[6], part), 71), part),
        "w_out": normal_values(streams_of[5], (D, D), D ** -0.5, 0.0625, ((0, 16),)),
    }


def apply_steer(queries, steer_ids, steer_table):
    lookup_ids = jnp.arange(steer_table.shape[0], dtype=jnp.int32)
    one_hot = (steer_ids[:, None] == lookup_ids[None, :]).astype(jnp.bfloat16)
    lookup = jnp.dot(one_hot, steer_table, preferred_element_type=jnp.float32)
    return (queries.astype(jnp.float32) + lookup).astype(jnp.bfloat16)


def local_keep(blocks, first_block, block_count, query_count):
    block_ids = first_block + jnp.arange(block_count, dtype=jnp.int32)
    hits = jnp.any(blocks[:, :, None] == block_ids[None, None, :], axis=1)
    full = jnp.broadcast_to(hits[:, None, :, None], (query_count // BLOCK, BLOCK, block_count, BLOCK))
    return full.reshape(query_count, block_count * BLOCK)


def group_attend(q_rows, k_rows, v_rows, keep_rows):
    scores = lax.dot_general(q_rows, k_rows, (((1,), (1,)), ((), ())), preferred_element_type=jnp.float32)
    scores = scores * (HEAD ** -0.5)
    masked = jnp.where(keep_rows, scores, jnp.float32(-1e30))
    row_peak = jnp.max(masked, axis=1)
    weights = jnp.where(keep_rows, jnp.exp(masked - row_peak[:, None]), jnp.float32(0.0))
    row_total = jnp.sum(weights, axis=1)
    probs = weights.astype(jnp.bfloat16)
    partial_out = jnp.dot(probs, v_rows, preferred_element_type=jnp.float32)
    return row_peak, row_total, partial_out


def partial_attention(steered, kv_piece, keep_mask):
    query_count = steered.shape[0]
    ctx_count = kv_piece.shape[1]
    group_size = HEADS // KV_HEADS
    q_groups = steered.reshape(query_count, KV_HEADS, group_size, HEAD).transpose(1, 2, 0, 3)
    q_groups = q_groups.reshape(KV_HEADS, group_size * query_count, HEAD)
    k_groups = kv_piece[0].reshape(ctx_count, KV_HEADS, HEAD).transpose(1, 0, 2)
    v_groups = kv_piece[1].reshape(ctx_count, KV_HEADS, HEAD).transpose(1, 0, 2)
    keep_rows = jnp.tile(keep_mask, (group_size, 1))

    def one_group(triple):
        return group_attend(triple[0], triple[1], triple[2], keep_rows)

    peaks, totals, outs = lax.map(one_group, (q_groups, k_groups, v_groups))
    peaks = peaks.reshape(KV_HEADS, group_size, query_count).transpose(2, 0, 1).reshape(query_count, HEADS)
    totals = totals.reshape(KV_HEADS, group_size, query_count).transpose(2, 0, 1).reshape(query_count, HEADS)
    outs = outs.reshape(KV_HEADS, group_size, query_count, HEAD).transpose(2, 0, 1, 3).reshape(query_count, HEADS * HEAD)
    return peaks, totals, outs


def reference(queries, steer_ids, steer_table, kv, blocks, w_out):
    steered = apply_steer(queries, steer_ids, steer_table)
    query_count = steered.shape[0]

    def visit(carry, shard_index):
        run_max, run_den, run_num = carry
        kv_piece = lax.dynamic_slice_in_dim(kv, shard_index * CTX_DEV, CTX_DEV, 1)
        keep_mask = local_keep(blocks, shard_index * BLOCKS_DEV, BLOCKS_DEV, query_count)
        peaks, totals, outs = partial_attention(steered, kv_piece, keep_mask)
        new_max = jnp.maximum(run_max, peaks)
        old_scale = jnp.exp(run_max - new_max)
        new_scale = jnp.exp(peaks - new_max)
        run_den = run_den * old_scale + totals * new_scale
        run_num = run_num * jnp.repeat(old_scale, HEAD, axis=1) + outs * jnp.repeat(new_scale, HEAD, axis=1)
        return (new_max, run_den, run_num), None

    start = (jnp.full((query_count, HEADS), -1e30, jnp.float32), jnp.zeros((query_count, HEADS), jnp.float32), jnp.zeros((query_count, HEADS * HEAD), jnp.float32))
    final, unused = lax.scan(visit, start, jnp.arange(N_CTX, dtype=jnp.int32))
    attended = (final[2] / jnp.repeat(final[1], HEAD, axis=1)).astype(jnp.bfloat16)
    return jnp.dot(attended, w_out, preferred_element_type=jnp.float32).astype(jnp.bfloat16)
```

```python
import jax
import jax.numpy as jnp
from jax import lax
from jax.experimental import pallas as pl
from jax.experimental.pallas import tpu as pltpu
from jax.sharding import PartitionSpec as P

HEADS = 64
KV_HEADS = 8
HEAD = 128
D = 8192
BLOCK = 64


def apply_steer(queries, steer_ids, steer_table):
    lookup_ids = jnp.arange(steer_table.shape[0], dtype=jnp.int32)
    one_hot = (steer_ids[:, None] == lookup_ids[None, :]).astype(jnp.bfloat16)
    lookup = jnp.dot(one_hot, steer_table, preferred_element_type=jnp.float32)
    return (queries.astype(jnp.float32) + lookup).astype(jnp.bfloat16)


def local_keep(blocks, first_block, block_count, query_count):
    block_ids = first_block + jnp.arange(block_count, dtype=jnp.int32)
    hits = jnp.any(blocks[:, :, None] == block_ids[None, None, :], axis=1)
    full = jnp.broadcast_to(
        hits[:, None, :, None], (query_count // BLOCK, BLOCK, block_count, BLOCK)
    )
    return full.reshape(query_count, block_count * BLOCK)


def group_attend(q_rows, k_rows, v_rows, keep_rows):
    scores = lax.dot_general(
        q_rows, k_rows, (((1,), (1,)), ((), ())), preferred_element_type=jnp.float32
    )
    scores = scores * HEAD ** (-0.5)
    masked = jnp.where(keep_rows, scores, jnp.float32(-1e30))
    row_peak = jnp.max(masked, axis=1)
    weights = jnp.where(keep_rows, jnp.exp(masked - row_peak[:, None]), jnp.float32(0.0))
    row_total = jnp.sum(weights, axis=1)
    probs = weights.astype(jnp.bfloat16)
    partial_out = jnp.dot(probs, v_rows, preferred_element_type=jnp.float32)
    return (row_peak, row_total, partial_out)


def partial_attention(steered, kv_piece, keep_mask):
    query_count = steered.shape[0]
    ctx_count = kv_piece.shape[1]
    group_size = HEADS // KV_HEADS
    q_groups = steered.reshape(query_count, KV_HEADS, group_size, HEAD).transpose(1, 2, 0, 3)
    q_groups = q_groups.reshape(KV_HEADS, group_size * query_count, HEAD)
    k_groups = kv_piece[0].reshape(ctx_count, KV_HEADS, HEAD).transpose(1, 0, 2)
    v_groups = kv_piece[1].reshape(ctx_count, KV_HEADS, HEAD).transpose(1, 0, 2)
    keep_rows = jnp.tile(keep_mask, (group_size, 1))

    def one_group(triple):
        return group_attend(triple[0], triple[1], triple[2], keep_rows)

    peaks, totals, outs = lax.map(one_group, (q_groups, k_groups, v_groups))
    peaks = (
        peaks.reshape(KV_HEADS, group_size, query_count)
        .transpose(2, 0, 1)
        .reshape(query_count, HEADS)
    )
    totals = (
        totals.reshape(KV_HEADS, group_size, query_count)
        .transpose(2, 0, 1)
        .reshape(query_count, HEADS)
    )
    outs = (
        outs.reshape(KV_HEADS, group_size, query_count, HEAD)
        .transpose(2, 0, 1, 3)
        .reshape(query_count, HEADS * HEAD)
    )
    return (peaks, totals, outs)


def per_device(queries, steer_ids, steer_table, kv, blocks, w_out):
    steered_local = apply_steer(queries, steer_ids, steer_table)
    steered = lax.all_gather(steered_local, "ctx", axis=0, tiled=True)
    shard_count = lax.axis_size("ctx")
    my_index = lax.axis_index("ctx")
    query_count = steered.shape[0]
    block_count = kv.shape[1] // BLOCK
    keep_mask = local_keep(blocks, my_index * block_count, block_count, query_count)
    peaks, totals, outs = partial_attention(steered, kv, keep_mask)
    stat_width = max(HEADS, shard_count)
    per_entry = D // stat_width
    col_count = D // shard_count

    def spread(values):
        return jnp.repeat(values, stat_width // HEADS, axis=1)

    got_num, got_max, got_den = (
        lax.all_to_all(outs, "ctx", split_axis=1, concat_axis=0, tiled=True),
        lax.all_to_all(spread(peaks), "ctx", split_axis=1, concat_axis=0, tiled=True),
        lax.all_to_all(spread(totals), "ctx", split_axis=1, concat_axis=0, tiled=True),
    )
    got_num = got_num.reshape(shard_count, query_count, col_count)
    got_max = got_max.reshape(shard_count, query_count, stat_width // shard_count)
    got_den = got_den.reshape(shard_count, query_count, stat_width // shard_count)
    overall = jnp.max(got_max, axis=0)
    scales = jnp.exp(got_max - overall[None])
    denominator = jnp.sum(scales * got_den, axis=0)
    numerator = jnp.sum(jnp.repeat(scales, per_entry, axis=2) * got_num, axis=0)
    attended = (numerator / jnp.repeat(denominator, per_entry, axis=1)).astype(jnp.bfloat16)
    return lax.psum_scatter(
        jnp.dot(attended, w_out, preferred_element_type=jnp.float32),
        "ctx",
        scatter_dimension=0,
        tiled=True,
    ).astype(jnp.bfloat16)


MESH = pl.DeviceIdType.MESH
EXP_SCALE = HEAD ** (-0.5) * 1.4426950408889634
GROUP = HEADS // KV_HEADS
OWN = GROUP // 2
CHUNKS = 4
CHUNK_COLS = D // CHUNKS
TILE = CHUNK_COLS // 2


def fused_kernel(
    q_ref, ids_ref, table_ref, blocks_ref, kv_hbm, w_hbm, out_ref,
    kv_ref, w_ref, q_all, bias_ref, q_rows, v_t,
    o_loc, s_loc, r1, rs1, t1, ts1, r2, rs2, t2, ts2, r3, rs3, t3, ts3, r4, rs4,
    att, p0, pr1, p1, pr2, p2, pr3, p3, pr4,
    kv_sem, w_sem, ag_send, ag_recv, rs_send, rs_recv, ss_send, ss_recv, pj_send, pj_recv,
):
    me = lax.axis_index("ctx")
    core = me % 2
    y = (me // 2) % 2
    z0 = (me // 4) % 2
    z1 = me // 8
    to_core = me + 1 - 2 * core
    to_y = me + 2 - 4 * y
    to_z0 = me + 4 - 8 * z0
    to_z1 = me + 8 - 16 * z1
    groups = q_all.shape[0]
    rows = q_ref.shape[0]
    keys = kv_ref.shape[1]
    key_blocks = keys // BLOCK
    queries = rows * 2 * groups

    kv_load = pltpu.make_async_copy(kv_hbm, kv_ref, kv_sem)
    w_load = pltpu.make_async_copy(w_hbm, w_ref, w_sem)
    kv_load.start()
    w_load.start()

    barrier = pltpu.get_barrier_semaphore()
    for other in (to_core, to_y, to_z0, to_z1):
        pl.semaphore_signal(barrier, inc=1, device_id={"ctx": other}, device_id_type=MESH)

    lookup_ids = lax.broadcasted_iota(jnp.int32, (rows, table_ref.shape[0]), 1)
    one_hot = jnp.where(ids_ref[...] == lookup_ids, 1.0, 0.0).astype(jnp.bfloat16)
    for g in range(groups):
        cols = slice(g * GROUP * HEAD, (g + 1) * GROUP * HEAD)
        lookup = jnp.dot(one_hot, table_ref[:, cols], preferred_element_type=jnp.float32)
        steered = q_ref[:, cols].astype(jnp.float32) + lookup
        stacked = jnp.concatenate(
            [steered[:, h * HEAD:(h + 1) * HEAD] for h in range(GROUP)], axis=0
        )
        q_all[g, z1, z0, y, core] = stacked.astype(jnp.bfloat16)

    def remote(src, dst, send, recv, other):
        return pltpu.make_async_remote_copy(
            src_ref=src, dst_ref=dst, send_sem=send, recv_sem=recv,
            device_id={"ctx": other}, device_id_type=MESH,
        )

    def gather(step, g):
        if step == 0:
            ref, other = q_all.at[g, z1, z0, y, core], to_z1
        elif step == 1:
            ref, other = q_all.at[g, :, z0, y, core], to_z0
        elif step == 2:
            ref, other = q_all.at[g, :, :, y, core], to_y
        else:
            ref, other = q_all.at[g, :, :, :, core], to_core
        return remote(ref, ref, ag_send.at[step, g], ag_recv.at[step, g], other)

    def merge_copies(step, i):
        if step == 0:
            a, b = (o_loc.at[i, 1 - core], r1.at[i]), (s_loc.at[i, 1 - core], rs1.at[i])
            other = to_core
        elif step == 1:
            a, b = (t1.at[2 * i + 1 - y], r2.at[i]), (ts1.at[2 * i + 1 - y], rs2.at[i])
            other = to_y
        elif step == 2:
            a, b = (t2.at[2 * i + 1 - z0], r3.at[i]), (ts2.at[2 * i + 1 - z0], rs3.at[i])
            other = to_z0
        else:
            a, b = (t3.at[1 - z1], r4.at[i]), (ts3.at[1 - z1], rs4.at[i])
            other = to_z1
        return (
            remote(a[0], a[1], rs_send.at[step, i], rs_recv.at[step, i], other),
            remote(b[0], b[1], ss_send.at[step, i], ss_recv.at[step, i], other),
        )

    def start_merge(step, i):
        for copy in merge_copies(step, i):
            copy.start()

    def wait_merge(step, i):
        for copy in merge_copies(step, i):
            copy.wait_recv()

    def merge_stats(sa, sb):
        ma, mb = sa[:OWN], sb[:OWN]
        peak = jnp.maximum(ma, mb)
        wa = jnp.exp2((ma - peak) * EXP_SCALE)
        wb = jnp.exp2((mb - peak) * EXP_SCALE)
        return peak, wa, wb, wa * sa[OWN:] + wb * sb[OWN:]

    def merge(oa, sa, ob, sb, o_dst, s_dst):
        peak, wa, wb, total = merge_stats(sa[...], sb[...])
        s_dst[...] = jnp.concatenate([peak, total], axis=0)
        for h in range(OWN):
            o_dst[h] = (
                oa[h].astype(jnp.float32) * wa[h:h + 1]
                + ob[h].astype(jnp.float32) * wb[h:h + 1]
            ).astype(jnp.bfloat16)

    first = me * key_blocks
    block_ids = first + lax.broadcasted_iota(jnp.int32, (key_blocks, blocks_ref.shape[1]), 0)
    lane_block = (lax.broadcasted_iota(jnp.int32, (key_blocks, 2 * queries), 1) % queries) // BLOCK
    bias = jnp.zeros((key_blocks, 2 * queries), jnp.float32)
    for b in range(blocks_ref.shape[0]):
        same = jnp.where(block_ids == blocks_ref[b:b + 1, :], 1.0, 0.0)
        hit = jnp.max(same, axis=1, keepdims=True)
        bias = jnp.where(lane_block == b, (hit - 1.0) * 1e30, bias)
    bias_ref[...] = bias

    pl.semaphore_wait(barrier, 4)

    @pl.loop(0, groups)
    def _(g):
        gather(0, g).start()

    kv_load.wait()

    def attend(g):
        lanes = pl.ds(pl.multiple_of(g * HEAD, HEAD), HEAD)
        v_t[...] = kv_ref[1, :, lanes].T
        q_wide = q_all[g].reshape(2 * groups, GROUP * rows, HEAD).astype(jnp.float32)
        for h in range(GROUP):
            head_rows = q_wide[:, h * rows:(h + 1) * rows, :].reshape(queries, HEAD)
            q_rows[h // 2, (h % 2) * queries:(h % 2 + 1) * queries] = head_rows.astype(jnp.bfloat16)

        @pl.loop(0, GROUP // 2)
        def _(hp):
            scores = lax.dot_general(
                kv_ref[0, :, lanes], q_rows[hp], (((1,), (1,)), ((), ())),
                preferred_element_type=jnp.float32,
            )
            scores = scores.reshape(key_blocks, BLOCK, 2 * queries) + bias_ref[...][:, None, :]
            scores = scores.reshape(keys, 2 * queries)
            peak = jnp.max(scores, axis=0, keepdims=True)
            weights = jnp.exp2((scores - peak) * EXP_SCALE)
            total = jnp.sum(weights, axis=0, keepdims=True)
            part = jnp.dot(v_t[...], weights.astype(jnp.bfloat16), preferred_element_type=jnp.float32)
            half = hp // (OWN // 2)
            base = (hp % (OWN // 2)) * 2
            for i in range(2):
                lane = slice(i * queries, (i + 1) * queries)
                o_loc[g, half, base + i] = part[:, lane].astype(jnp.bfloat16)
                s_loc[g, half, pl.ds(base + i, 1), :] = peak[:, lane]
                s_loc[g, half, pl.ds(OWN + base + i, 1), :] = total[:, lane]

    def at(cond, fn):
        pl.when(cond)(fn)

    @pl.loop(0, groups + 6)
    def _(t):
        for step in range(3):
            def advance(step=step):
                gather(step, t - step).wait_recv()
                gather(step + 1, t - step).start()
            at((t >= step) & (t < groups + step), advance)

        def attention():
            g = t - 3
            gather(3, g).wait_recv()
            attend(g)
            start_merge(0, g)
        at((t >= 3) & (t < groups + 3), attention)

        def merge_core():
            g = t - 4
            wait_merge(0, g)
            merge(o_loc.at[g, core], s_loc.at[g, core], r1.at[g], rs1.at[g], t1.at[g], ts1.at[g])
            at(g % 2 == 1, lambda: start_merge(1, g // 2))
        at((t >= 4) & (t < groups + 4), merge_core)

        def merge_y():
            j = (t - 5) // 2
            wait_merge(1, j)
            merge(t1.at[2 * j + y], ts1.at[2 * j + y], r2.at[j], rs2.at[j], t2.at[j], ts2.at[j])
            at(j % 2 == 1, lambda: start_merge(2, j // 2))
        at((t >= 6) & (t < groups + 5) & (t % 2 == 0), merge_y)

        def merge_z0():
            k = (t - 6) // 4
            wait_merge(2, k)
            merge(t2.at[2 * k + z0], ts2.at[2 * k + z0], r3.at[k], rs3.at[k], t3.at[k], ts3.at[k])
        at((t >= 9) & (t < groups + 6) & (t % 4 == 1), merge_z0)

    start_merge(3, 0)
    w_load.wait()
    wait_merge(3, 0)
    peak, wa, wb, total = merge_stats(ts3[z1], rs4[0])
    inverse = 1.0 / total
    wa, wb = wa * inverse, wb * inverse
    for h in range(OWN):
        done = t3[z1, h].astype(jnp.float32) * wa[h:h + 1] + r4[0, h].astype(jnp.float32) * wb[h:h + 1]
        att[:, h * HEAD:(h + 1) * HEAD] = done.T.astype(jnp.bfloat16)

    def project_copy(step, c):
        swap = c % 2 == 1
        if step == 0:
            src, dst, other = p0.at[c, :, :, :, 1 - core], pr1.at[c], to_core
        elif step == 1:
            src = p1.at[c, :, 1 - z0] if swap else p1.at[c, :, :, 1 - y]
            dst, other = pr2.at[c], to_z0 if swap else to_y
        elif step == 2:
            src = p2.at[c, :, 1 - y] if swap else p2.at[c, :, 1 - z0]
            dst, other = pr3.at[c], to_y if swap else to_z0
        else:
            src, dst, other = p3.at[c, 1 - z1], pr4.at[c], to_z1
        return remote(src, dst, pj_send.at[step, c], pj_recv.at[step, c], other)

    def add(a, b):
        return (a.astype(jnp.float32) + b.astype(jnp.float32)).astype(jnp.bfloat16)

    def stage(step, c):
        swap = c % 2 == 1
        if step == 0:
            halves = []
            for i in range(2):
                base = c * CHUNK_COLS + i * TILE
                part = jnp.dot(att[...], w_ref[:, base:base + TILE], preferred_element_type=jnp.float32)
                halves.append(part.reshape(2 * groups, rows, TILE))
            both = jnp.concatenate(halves, axis=1).astype(jnp.bfloat16)
            p0[c] = both.reshape(2, 2, 2, 2, 2 * rows, TILE)
        else:
            project_copy(step - 1, c).wait_recv()
            if step == 1:
                p1[c] = add(p0[c, :, :, :, core], pr1[c])
            elif step == 2:
                p2[c] = add(p1[c, :, z0] if swap else p1[c, :, :, y], pr2[c])
            elif step == 3:
                p3[c] = add(p2[c, :, y] if swap else p2[c, :, z0], pr3[c])
            else:
                done = p3[c, z1].astype(jnp.float32) + pr4[c].astype(jnp.float32)
                for i in range(2):
                    base = c * CHUNK_COLS + i * TILE
                    out_ref[:, base:base + TILE] = done[i * rows:(i + 1) * rows].astype(jnp.bfloat16)
        if step < 4:
            project_copy(step, c).start()

    for t in range(CHUNKS + 4):
        for step in range(5):
            if 0 <= t - step < CHUNKS:
                stage(step, t - step)

    @pl.loop(0, groups)
    def _(g):
        for step in range(4):
            gather(step, g).wait_send()

    for step in range(4):
        for i in range(groups >> step):
            for copy in merge_copies(step, i):
                copy.wait_send()
        for c in range(CHUNKS):
            project_copy(step, c).wait_send()


def per_device_fused(queries, steer_ids, steer_table, kv, blocks, w_out):
    rows = queries.shape[0]
    keys = kv.shape[1]
    groups = KV_HEADS
    total_q = 2 * groups * rows
    bf, f32 = jnp.bfloat16, jnp.float32
    piece = (OWN, HEAD, total_q)
    stat = (2 * OWN, total_q)
    tile = (2 * rows, TILE)
    scratch = [
        pltpu.VMEM(kv.shape, bf),
        pltpu.VMEM(w_out.shape, bf),
        pltpu.VMEM((groups, 2, 2, 2, 2, GROUP * rows, HEAD), bf),
        pltpu.VMEM((keys // BLOCK, 2 * total_q), f32),
        pltpu.VMEM((GROUP // 2, 2 * total_q, HEAD), bf),
        pltpu.VMEM((HEAD, keys), bf),
        pltpu.VMEM((groups, 2) + piece, bf),
        pltpu.VMEM((groups, 2) + stat, f32),
    ]
    for count in (groups, groups // 2, groups // 4):
        scratch += [
            pltpu.VMEM((count,) + piece, bf), pltpu.VMEM((count,) + stat, f32),
            pltpu.VMEM((count,) + piece, bf), pltpu.VMEM((count,) + stat, f32),
        ]
    scratch += [pltpu.VMEM((1,) + piece, bf), pltpu.VMEM((1,) + stat, f32)]
    scratch += [
        pltpu.VMEM((total_q, OWN * HEAD), bf),
        pltpu.VMEM((CHUNKS, 2, 2, 2, 2) + tile, bf),
    ]
    for lead in ((2, 2, 2), (2, 2), (2,)):
        scratch += [pltpu.VMEM((CHUNKS,) + lead + tile, bf), pltpu.VMEM((CHUNKS,) + lead + tile, bf)]
    scratch += [pltpu.VMEM((CHUNKS,) + tile, bf)]
    dma = pltpu.SemaphoreType.DMA
    scratch += [dma(()), dma(())] + [dma((4, groups))] * 6 + [dma((4, CHUNKS))] * 2
    vmem = pl.BlockSpec(memory_space=pltpu.VMEM)
    hbm = pl.BlockSpec(memory_space=pl.ANY)
    return pl.pallas_call(
        fused_kernel,
        out_shape=jax.ShapeDtypeStruct(queries.shape, bf),
        in_specs=[vmem, vmem, vmem, vmem, hbm, hbm],
        out_specs=vmem,
        scratch_shapes=scratch,
        compiler_params=pltpu.CompilerParams(
            collective_id=0, has_side_effects=True, vmem_limit_bytes=48 * 1024 * 1024
        ),
    )(queries, steer_ids[:, None], steer_table, blocks, kv, w_out)


def solution(mesh):
    fits = mesh.shape["ctx"] == 2 * KV_HEADS
    return jax.shard_map(
        per_device_fused if fits else per_device,
        mesh=mesh,
        in_specs=(
            P(("parts", "ctx"), None),
            P(("parts", "ctx")),
            P(),
            P(None, ("parts", "ctx"), None),
            P("parts", None),
            P("ctx", None),
        ),
        out_specs=P(("parts", "ctx"), None),
        check_vma=False,
    )
```

```python
import jax
import jax.numpy as jnp
from jax import lax
from jax.experimental import pallas as pl
from jax.experimental.pallas import tpu as pltpu
from jax.sharding import PartitionSpec as P

HEADS = 64
KV_HEADS = 8
HEAD = 128
D = 8192
BLOCK = 64


def apply_steer(queries, steer_ids, steer_table):
    lookup_ids = jnp.arange(steer_table.shape[0], dtype=jnp.int32)
    one_hot = (steer_ids[:, None] == lookup_ids[None, :]).astype(jnp.bfloat16)
    lookup = jnp.dot(one_hot, steer_table, preferred_element_type=jnp.float32)
    return (queries.astype(jnp.float32) + lookup).astype(jnp.bfloat16)


def local_keep(blocks, first_block, block_count, query_count):
    block_ids = first_block + jnp.arange(block_count, dtype=jnp.int32)
    hits = jnp.any(blocks[:, :, None] == block_ids[None, None, :], axis=1)
    full = jnp.broadcast_to(
        hits[:, None, :, None], (query_count // BLOCK, BLOCK, block_count, BLOCK)
    )
    return full.reshape(query_count, block_count * BLOCK)


def group_attend(q_rows, k_rows, v_rows, keep_rows):
    scores = lax.dot_general(
        q_rows, k_rows, (((1,), (1,)), ((), ())), preferred_element_type=jnp.float32
    )
    scores = scores * HEAD ** (-0.5)
    masked = jnp.where(keep_rows, scores, jnp.float32(-1e30))
    row_peak = jnp.max(masked, axis=1)
    weights = jnp.where(keep_rows, jnp.exp(masked - row_peak[:, None]), jnp.float32(0.0))
    row_total = jnp.sum(weights, axis=1)
    probs = weights.astype(jnp.bfloat16)
    partial_out = jnp.dot(probs, v_rows, preferred_element_type=jnp.float32)
    return (row_peak, row_total, partial_out)


def partial_attention(steered, kv_piece, keep_mask):
    query_count = steered.shape[0]
    ctx_count = kv_piece.shape[1]
    group_size = HEADS // KV_HEADS
    q_groups = steered.reshape(query_count, KV_HEADS, group_size, HEAD).transpose(1, 2, 0, 3)
    q_groups = q_groups.reshape(KV_HEADS, group_size * query_count, HEAD)
    k_groups = kv_piece[0].reshape(ctx_count, KV_HEADS, HEAD).transpose(1, 0, 2)
    v_groups = kv_piece[1].reshape(ctx_count, KV_HEADS, HEAD).transpose(1, 0, 2)
    keep_rows = jnp.tile(keep_mask, (group_size, 1))

    def one_group(triple):
        return group_attend(triple[0], triple[1], triple[2], keep_rows)

    peaks, totals, outs = lax.map(one_group, (q_groups, k_groups, v_groups))
    peaks = (
        peaks.reshape(KV_HEADS, group_size, query_count)
        .transpose(2, 0, 1)
        .reshape(query_count, HEADS)
    )
    totals = (
        totals.reshape(KV_HEADS, group_size, query_count)
        .transpose(2, 0, 1)
        .reshape(query_count, HEADS)
    )
    outs = (
        outs.reshape(KV_HEADS, group_size, query_count, HEAD)
        .transpose(2, 0, 1, 3)
        .reshape(query_count, HEADS * HEAD)
    )
    return (peaks, totals, outs)


def per_device(queries, steer_ids, steer_table, kv, blocks, w_out):
    steered_local = apply_steer(queries, steer_ids, steer_table)
    steered = lax.all_gather(steered_local, "ctx", axis=0, tiled=True)
    shard_count = lax.axis_size("ctx")
    my_index = lax.axis_index("ctx")
    query_count = steered.shape[0]
    block_count = kv.shape[1] // BLOCK
    keep_mask = local_keep(blocks, my_index * block_count, block_count, query_count)
    peaks, totals, outs = partial_attention(steered, kv, keep_mask)
    stat_width = max(HEADS, shard_count)
    per_entry = D // stat_width
    col_count = D // shard_count

    def spread(values):
        return jnp.repeat(values, stat_width // HEADS, axis=1)

    got_num, got_max, got_den = (
        lax.all_to_all(outs, "ctx", split_axis=1, concat_axis=0, tiled=True),
        lax.all_to_all(spread(peaks), "ctx", split_axis=1, concat_axis=0, tiled=True),
        lax.all_to_all(spread(totals), "ctx", split_axis=1, concat_axis=0, tiled=True),
    )
    got_num = got_num.reshape(shard_count, query_count, col_count)
    got_max = got_max.reshape(shard_count, query_count, stat_width // shard_count)
    got_den = got_den.reshape(shard_count, query_count, stat_width // shard_count)
    overall = jnp.max(got_max, axis=0)
    scales = jnp.exp(got_max - overall[None])
    denominator = jnp.sum(scales * got_den, axis=0)
    numerator = jnp.sum(jnp.repeat(scales, per_entry, axis=2) * got_num, axis=0)
    attended = (numerator / jnp.repeat(denominator, per_entry, axis=1)).astype(jnp.bfloat16)
    return lax.psum_scatter(
        jnp.dot(attended, w_out, preferred_element_type=jnp.float32),
        "ctx",
        scatter_dimension=0,
        tiled=True,
    ).astype(jnp.bfloat16)


MESH = pl.DeviceIdType.MESH
EXP_SCALE = HEAD ** (-0.5) * 1.4426950408889634
GROUP = HEADS // KV_HEADS
OWN = GROUP // 2
CHUNKS = 4
CHUNK_COLS = D // CHUNKS
TILE = CHUNK_COLS // 2


def fused_kernel(
    q_ref, ids_hbm, table_hbm, blocks_hbm, kv_hbm, w_hbm, out_ref,
    ids_ref, table_ref, blocks_ref, kv_ref, w_ref, q_all, bias_ref, q_rows, v_t,
    o_send, s_send, o_keep, s_keep, r1, rs1,
    t1s, ts1s, t1k, ts1k, r2, rs2,
    t2s, ts2s, t2k, ts2k, r3, rs3,
    t3s, ts3s, t3k, ts3k, r4, rs4,
    att, p0, p0s, pr1, p1, p1s, pr2, p2, p2s, pr3, p3, p3s, pr4,
    ids_sem, table_sem, blocks_sem, kv_sem, w_sem,
    ag_send, ag_recv, rs_send, rs_recv, ss_send, ss_recv, pj_send, pj_recv,
):
    me = lax.axis_index("ctx")
    core = me % 2
    y = (me // 2) % 2
    z0 = (me // 4) % 2
    z1 = me // 8
    to_core = me + 1 - 2 * core
    to_y = me + 2 - 4 * y
    to_z0 = me + 4 - 8 * z0
    to_z1 = me + 8 - 16 * z1
    groups = q_all.shape[0]
    rows = q_ref.shape[0]
    keys = kv_ref.shape[1]
    key_blocks = keys // BLOCK
    queries = rows * 2 * groups

    kv_load = pltpu.make_async_copy(kv_hbm, kv_ref, kv_sem)
    w_load = pltpu.make_async_copy(w_hbm, w_ref, w_sem)
    ids_load = pltpu.make_async_copy(ids_hbm, ids_ref, ids_sem)
    table_load = pltpu.make_async_copy(table_hbm, table_ref, table_sem)
    blocks_load = pltpu.make_async_copy(blocks_hbm, blocks_ref, blocks_sem)
    for load in (ids_load, table_load, blocks_load, kv_load, w_load):
        load.start()

    barrier = pltpu.get_barrier_semaphore()
    for other in (to_core, to_y, to_z0, to_z1):
        pl.semaphore_signal(barrier, inc=1, device_id={"ctx": other}, device_id_type=MESH)

    ids_load.wait()
    table_load.wait()
    blocks_load.wait()
    row_at = lax.broadcasted_iota(jnp.int32, (rows, rows), 0)
    lane_at = lax.broadcasted_iota(jnp.int32, (rows, rows), 1)
    ids_wide = jnp.broadcast_to(ids_ref[...].astype(jnp.float32), (rows, rows))
    ids_col = jnp.sum(jnp.where(row_at == lane_at, ids_wide, 0.0), axis=1, keepdims=True)
    lookup_ids = lax.broadcasted_iota(jnp.int32, (rows, table_ref.shape[0]), 1)
    one_hot = jnp.where(ids_col == lookup_ids.astype(jnp.float32), 1.0, 0.0).astype(jnp.bfloat16)
    for g in range(groups):
        cols = slice(g * GROUP * HEAD, (g + 1) * GROUP * HEAD)
        lookup = jnp.dot(one_hot, table_ref[:, cols], preferred_element_type=jnp.float32)
        steered = q_ref[:, cols].astype(jnp.float32) + lookup
        stacked = jnp.concatenate(
            [steered[:, h * HEAD:(h + 1) * HEAD] for h in range(GROUP)], axis=0
        )
        q_all[g, z1, z0, y, core] = stacked.astype(jnp.bfloat16)

    def remote(src, dst, send, recv, other):
        return pltpu.make_async_remote_copy(
            src_ref=src, dst_ref=dst, send_sem=send, recv_sem=recv,
            device_id={"ctx": other}, device_id_type=MESH,
        )

    def gather(step, g):
        if step == 0:
            ref, other = q_all.at[g, z1, z0, y, core], to_z1
        elif step == 1:
            ref, other = q_all.at[g, :, z0, y, core], to_z0
        elif step == 2:
            ref, other = q_all.at[g, :, :, y, core], to_y
        else:
            ref, other = q_all.at[g, :, :, :, core], to_core
        return remote(ref, ref, ag_send.at[step, g], ag_recv.at[step, g], other)

    def pick(mine, bit):
        return mine * bit + (1 - mine) * (1 - bit)

    def order(step, p):
        a = z1 if step >= 1 else 1 - z1
        b = z0 if step >= 2 else 1 - z0
        c = y if step >= 3 else 1 - y
        return 4 * pick(a, p // 4) + 2 * pick(b, (p // 2) % 2) + pick(c, p % 2)

    def merge_copies(step, i):
        if step == 0:
            a, b, other = (o_send.at[i], r1.at[i]), (s_send.at[i], rs1.at[i]), to_core
        elif step == 1:
            a, b, other = (t1s.at[i], r2.at[i]), (ts1s.at[i], rs2.at[i]), to_y
        elif step == 2:
            a, b, other = (t2s.at[i], r3.at[i]), (ts2s.at[i], rs3.at[i]), to_z0
        else:
            a, b, other = (t3s.at[i], r4.at[i]), (ts3s.at[i], rs4.at[i]), to_z1
        return (
            remote(a[0], a[1], rs_send.at[step, i], rs_recv.at[step, i], other),
            remote(b[0], b[1], ss_send.at[step, i], ss_recv.at[step, i], other),
        )

    def start_merge(step, i):
        for copy in merge_copies(step, i):
            copy.start()

    def wait_merge(step, i):
        for copy in merge_copies(step, i):
            copy.wait_recv()

    def merge_stats(sa, sb):
        ma, mb = sa[:OWN], sb[:OWN]
        peak = jnp.maximum(ma, mb)
        wa = jnp.exp2((ma - peak) * EXP_SCALE)
        wb = jnp.exp2((mb - peak) * EXP_SCALE)
        return peak, wa, wb, wa * sa[OWN:] + wb * sb[OWN:]

    def merge(oa, sa, ob, sb, o_dst, s_dst):
        peak, wa, wb, total = merge_stats(sa[...], sb[...])
        s_dst[...] = jnp.concatenate([peak, total], axis=0)
        for h in range(OWN):
            o_dst[h] = (
                oa[h].astype(jnp.float32) * wa[h:h + 1]
                + ob[h].astype(jnp.float32) * wb[h:h + 1]
            ).astype(o_dst.dtype)

    first = me * key_blocks
    block_ids = first + lax.broadcasted_iota(jnp.int32, (key_blocks, blocks_ref.shape[1]), 0)
    lane_block = (lax.broadcasted_iota(jnp.int32, (key_blocks, 2 * queries), 1) % queries) // BLOCK
    bias = jnp.zeros((key_blocks, 2 * queries), jnp.float32)
    for b in range(blocks_ref.shape[0]):
        same = jnp.where(block_ids == blocks_ref[b:b + 1, :], 1.0, 0.0)
        hit = jnp.max(same, axis=1, keepdims=True)
        bias = jnp.where(lane_block == b, (hit - 1.0) * 1e30, bias)
    bias_ref[...] = bias

    pl.semaphore_wait(barrier, 4)

    @pl.loop(0, groups)
    def _(p):
        gather(0, order(0, p)).start()

    kv_load.wait()

    def attend(g):
        lanes = pl.ds(pl.multiple_of(g * HEAD, HEAD), HEAD)
        v_t[...] = kv_ref[1, :, lanes].T
        q_wide = q_all[g].reshape(2 * groups, GROUP * rows, HEAD).astype(jnp.float32)
        for h in range(GROUP):
            head_rows = q_wide[:, h * rows:(h + 1) * rows, :].reshape(queries, HEAD)
            q_rows[h // 2, (h % 2) * queries:(h % 2 + 1) * queries] = head_rows.astype(jnp.bfloat16)

        def heads(half, o_dst, s_dst):
            @pl.loop(0, OWN // 2)
            def _(i):
                scores = lax.dot_general(
                    kv_ref[0, :, lanes], q_rows[half * (OWN // 2) + i], (((1,), (1,)), ((), ())),
                    preferred_element_type=jnp.float32,
                )
                scores = scores.reshape(key_blocks, BLOCK, 2 * queries) + bias_ref[...][:, None, :]
                scores = scores.reshape(keys, 2 * queries)
                peak = jnp.max(scores, axis=0, keepdims=True)
                weights = jnp.exp2((scores - peak) * EXP_SCALE)
                total = jnp.sum(weights, axis=0, keepdims=True)
                part = jnp.dot(v_t[...], weights.astype(jnp.bfloat16), preferred_element_type=jnp.float32)
                for h in range(2):
                    lane = slice(h * queries, (h + 1) * queries)
                    o_dst[g, 2 * i + h] = part[:, lane].astype(o_dst.dtype)
                    s_dst[g, pl.ds(2 * i + h, 1), :] = peak[:, lane]
                    s_dst[g, pl.ds(OWN + 2 * i + h, 1), :] = total[:, lane]

        heads(1 - core, o_send, s_send)
        start_merge(0, g)
        heads(core, o_keep, s_keep)

    def at(cond, fn):
        pl.when(cond)(fn)

    @pl.loop(0, groups + 9)
    def _(t):
        for step in range(3):
            def advance(step=step):
                g = order(step + 1, t - 2 * step)
                gather(step, g).wait_recv()
                gather(step + 1, g).start()
            at((t >= 2 * step) & (t < groups + 2 * step), advance)

        def attention():
            g = order(3, t - 6)
            gather(3, g).wait_recv()
            attend(g)
        at((t >= 6) & (t < groups + 6), attention)

        def merge_core():
            p = t - 7
            g = order(3, p)
            j = g // 2
            wait_merge(0, g)
            parts = (o_keep.at[g], s_keep.at[g], r1.at[g], rs1.at[g])

            def send():
                merge(*parts, t1s.at[j], ts1s.at[j])
                start_merge(1, j)
            at(p % 2 == 0, send)
            at(p % 2 == 1, lambda: merge(*parts, t1k.at[j], ts1k.at[j]))
        at((t >= 7) & (t < groups + 7), merge_core)

        def merge_y():
            p = t - 8
            j = order(3, p) // 2
            k = j // 2
            wait_merge(1, j)
            parts = (t1k.at[j], ts1k.at[j], r2.at[j], rs2.at[j])

            def send():
                merge(*parts, t2s.at[k], ts2s.at[k])
                start_merge(2, k)
            at(p % 4 == 1, send)
            at(p % 4 == 3, lambda: merge(*parts, t2k.at[k], ts2k.at[k]))
        at((t >= 9) & (t < groups + 8) & (t % 2 == 1), merge_y)

        def merge_z0():
            p = t - 9
            k = order(3, p) // 4
            wait_merge(2, k)
            parts = (t2k.at[k], ts2k.at[k], r3.at[k], rs3.at[k])

            def send():
                merge(*parts, t3s.at[0], ts3s.at[0])
                start_merge(3, 0)
            at(p == 3, send)
            at(p == 7, lambda: merge(*parts, t3k.at[0], ts3k.at[0]))
        at((t == 12) | (t == 16), merge_z0)

    w_load.wait()
    wait_merge(3, 0)
    peak, wa, wb, total = merge_stats(ts3k[0], rs4[0])
    inverse = 1.0 / total
    wa, wb = wa * inverse, wb * inverse
    for h in range(OWN):
        done = t3k[0, h] * wa[h:h + 1] + r4[0, h].astype(jnp.float32) * wb[h:h + 1]
        att[:, h * HEAD:(h + 1) * HEAD] = done.T.astype(jnp.bfloat16)

    def project_copy(step, c):
        swap = c % 2 == 1
        if step == 0:
            src, dst, other = p0s.at[c], pr1.at[c], to_core
        elif step == 1:
            src, dst, other = p1s.at[c], pr2.at[c], to_z0 if swap else to_y
        elif step == 2:
            src, dst, other = p2s.at[c], pr3.at[c], to_y if swap else to_z0
        else:
            src, dst, other = p3s.at[c], pr4.at[c], to_z1
        return remote(src, dst, pj_send.at[step, c], pj_recv.at[step, c], other)

    def stage(step, c):
        swap = c % 2 == 1
        low = jnp.bfloat16
        if step > 0:
            project_copy(step - 1, c).wait_recv()
        if step == 0:
            halves = []
            for i in range(2):
                base = c * CHUNK_COLS + i * TILE
                part = jnp.dot(att[...], w_ref[:, base:base + TILE], preferred_element_type=jnp.float32)
                halves.append(part.reshape(2 * groups, rows, TILE))
            both = jnp.concatenate(halves, axis=1)
            p0[c] = both.reshape(2, 2, 2, 2, 2 * rows, TILE)
            p0s[c] = p0[c, :, :, :, 1 - core].astype(low)
        elif step == 1:
            p1[c] = p0[c, :, :, :, core] + pr1[c].astype(jnp.float32)
            p1s[c] = (p1[c, :, 1 - z0] if swap else p1[c, :, :, 1 - y]).astype(low)
        elif step == 2:
            p2[c] = (p1[c, :, z0] if swap else p1[c, :, :, y]) + pr2[c].astype(jnp.float32)
            p2s[c] = (p2[c, :, 1 - y] if swap else p2[c, :, 1 - z0]).astype(low)
        elif step == 3:
            p3[c] = (p2[c, :, y] if swap else p2[c, :, z0]) + pr3[c].astype(jnp.float32)
            p3s[c] = p3[c, 1 - z1].astype(low)
        else:
            done = p3[c, z1] + pr4[c].astype(jnp.float32)
            for i in range(2):
                base = c * CHUNK_COLS + i * TILE
                out_ref[:, base:base + TILE] = done[i * rows:(i + 1) * rows].astype(low)
        if step < 4:
            project_copy(step, c).start()

    for t in range(CHUNKS + 4):
        for step in range(5):
            if 0 <= t - step < CHUNKS:
                stage(step, t - step)

    @pl.loop(0, groups)
    def _(g):
        for step in range(4):
            gather(step, g).wait_send()

    for step in range(4):
        for i in range(max(groups >> step, 1)):
            for copy in merge_copies(step, i):
                copy.wait_send()
        for c in range(CHUNKS):
            project_copy(step, c).wait_send()


def per_device_fused(queries, steer_ids, steer_table, kv, blocks, w_out):
    rows = queries.shape[0]
    keys = kv.shape[1]
    groups = KV_HEADS
    total_q = 2 * groups * rows
    bf, f32 = jnp.bfloat16, jnp.float32
    piece = (OWN, HEAD, total_q)
    stat = (2 * OWN, total_q)
    tile = (2 * rows, TILE)
    scratch = [
        pltpu.VMEM((1, rows), jnp.int32),
        pltpu.VMEM(steer_table.shape, bf),
        pltpu.VMEM(blocks.shape, jnp.int32),
        pltpu.VMEM(kv.shape, bf),
        pltpu.VMEM(w_out.shape, bf),
        pltpu.VMEM((groups, 2, 2, 2, 2, GROUP * rows, HEAD), bf),
        pltpu.VMEM((keys // BLOCK, 2 * total_q), f32),
        pltpu.VMEM((GROUP // 2, 2 * total_q, HEAD), bf),
        pltpu.VMEM((HEAD, keys), bf),
    ]
    for count in (groups, groups // 2, groups // 4, groups // 8):
        for kind in (bf, f32, bf):
            scratch += [pltpu.VMEM((count,) + piece, kind), pltpu.VMEM((count,) + stat, f32)]
    scratch += [pltpu.VMEM((total_q, OWN * HEAD), bf), pltpu.VMEM((CHUNKS, 2, 2, 2, 2) + tile, f32)]
    for lead in ((2, 2, 2), (2, 2), (2,)):
        many = (CHUNKS,) + lead + tile
        scratch += [pltpu.VMEM(many, bf), pltpu.VMEM(many, bf), pltpu.VMEM(many, f32)]
    scratch += [pltpu.VMEM((CHUNKS,) + tile, bf), pltpu.VMEM((CHUNKS,) + tile, bf)]
    dma = pltpu.SemaphoreType.DMA
    scratch += [dma(())] * 5 + [dma((4, groups))] * 6 + [dma((4, CHUNKS))] * 2
    vmem = pl.BlockSpec(memory_space=pltpu.VMEM)
    hbm = pl.BlockSpec(memory_space=pl.ANY)
    return pl.pallas_call(
        fused_kernel,
        out_shape=jax.ShapeDtypeStruct(queries.shape, bf),
        in_specs=[vmem, hbm, hbm, hbm, hbm, hbm],
        out_specs=vmem,
        scratch_shapes=scratch,
        compiler_params=pltpu.CompilerParams(
            collective_id=0, has_side_effects=True, vmem_limit_bytes=48 * 1024 * 1024
        ),
    )(queries, steer_ids[None, :], steer_table, blocks, kv, w_out)


def solution(mesh):
    fits = mesh.shape["ctx"] == 2 * KV_HEADS
    return jax.shard_map(
        per_device_fused if fits else per_device,
        mesh=mesh,
        in_specs=(
            P(("parts", "ctx"), None),
            P(("parts", "ctx")),
            P(),
            P(None, ("parts", "ctx"), None),
            P("parts", None),
            P("ctx", None),
        ),
        out_specs=P(("parts", "ctx"), None),
        check_vma=False,
    )
```

```python
import jax
import jax.numpy as jnp
from jax import lax
from jax.experimental import pallas as pl
from jax.experimental.pallas import tpu as pltpu
from jax.sharding import PartitionSpec as P

HEADS = 64
KV_HEADS = 8
HEAD = 128
D = 8192
BLOCK = 64


def apply_steer(queries, steer_ids, steer_table):
    lookup_ids = jnp.arange(steer_table.shape[0], dtype=jnp.int32)
    one_hot = (steer_ids[:, None] == lookup_ids[None, :]).astype(jnp.bfloat16)
    lookup = jnp.dot(one_hot, steer_table, preferred_element_type=jnp.float32)
    return (queries.astype(jnp.float32) + lookup).astype(jnp.bfloat16)


def local_keep(blocks, first_block, block_count, query_count):
    block_ids = first_block + jnp.arange(block_count, dtype=jnp.int32)
    hits = jnp.any(blocks[:, :, None] == block_ids[None, None, :], axis=1)
    full = jnp.broadcast_to(
        hits[:, None, :, None], (query_count // BLOCK, BLOCK, block_count, BLOCK)
    )
    return full.reshape(query_count, block_count * BLOCK)


def group_attend(q_rows, k_rows, v_rows, keep_rows):
    scores = lax.dot_general(
        q_rows, k_rows, (((1,), (1,)), ((), ())), preferred_element_type=jnp.float32
    )
    scores = scores * HEAD ** (-0.5)
    masked = jnp.where(keep_rows, scores, jnp.float32(-1e30))
    row_peak = jnp.max(masked, axis=1)
    weights = jnp.where(keep_rows, jnp.exp(masked - row_peak[:, None]), jnp.float32(0.0))
    row_total = jnp.sum(weights, axis=1)
    probs = weights.astype(jnp.bfloat16)
    partial_out = jnp.dot(probs, v_rows, preferred_element_type=jnp.float32)
    return (row_peak, row_total, partial_out)


def partial_attention(steered, kv_piece, keep_mask):
    query_count = steered.shape[0]
    ctx_count = kv_piece.shape[1]
    group_size = HEADS // KV_HEADS
    q_groups = steered.reshape(query_count, KV_HEADS, group_size, HEAD).transpose(1, 2, 0, 3)
    q_groups = q_groups.reshape(KV_HEADS, group_size * query_count, HEAD)
    k_groups = kv_piece[0].reshape(ctx_count, KV_HEADS, HEAD).transpose(1, 0, 2)
    v_groups = kv_piece[1].reshape(ctx_count, KV_HEADS, HEAD).transpose(1, 0, 2)
    keep_rows = jnp.tile(keep_mask, (group_size, 1))

    def one_group(triple):
        return group_attend(triple[0], triple[1], triple[2], keep_rows)

    peaks, totals, outs = lax.map(one_group, (q_groups, k_groups, v_groups))
    peaks = (
        peaks.reshape(KV_HEADS, group_size, query_count)
        .transpose(2, 0, 1)
        .reshape(query_count, HEADS)
    )
    totals = (
        totals.reshape(KV_HEADS, group_size, query_count)
        .transpose(2, 0, 1)
        .reshape(query_count, HEADS)
    )
    outs = (
        outs.reshape(KV_HEADS, group_size, query_count, HEAD)
        .transpose(2, 0, 1, 3)
        .reshape(query_count, HEADS * HEAD)
    )
    return (peaks, totals, outs)


def per_device(queries, steer_ids, steer_table, kv, blocks, w_out):
    steered_local = apply_steer(queries, steer_ids, steer_table)
    steered = lax.all_gather(steered_local, "ctx", axis=0, tiled=True)
    shard_count = lax.axis_size("ctx")
    my_index = lax.axis_index("ctx")
    query_count = steered.shape[0]
    block_count = kv.shape[1] // BLOCK
    keep_mask = local_keep(blocks, my_index * block_count, block_count, query_count)
    peaks, totals, outs = partial_attention(steered, kv, keep_mask)
    stat_width = max(HEADS, shard_count)
    per_entry = D // stat_width
    col_count = D // shard_count

    def spread(values):
        return jnp.repeat(values, stat_width // HEADS, axis=1)

    got_num, got_max, got_den = (
        lax.all_to_all(outs, "ctx", split_axis=1, concat_axis=0, tiled=True),
        lax.all_to_all(spread(peaks), "ctx", split_axis=1, concat_axis=0, tiled=True),
        lax.all_to_all(spread(totals), "ctx", split_axis=1, concat_axis=0, tiled=True),
    )
    got_num = got_num.reshape(shard_count, query_count, col_count)
    got_max = got_max.reshape(shard_count, query_count, stat_width // shard_count)
    got_den = got_den.reshape(shard_count, query_count, stat_width // shard_count)
    overall = jnp.max(got_max, axis=0)
    scales = jnp.exp(got_max - overall[None])
    denominator = jnp.sum(scales * got_den, axis=0)
    numerator = jnp.sum(jnp.repeat(scales, per_entry, axis=2) * got_num, axis=0)
    attended = (numerator / jnp.repeat(denominator, per_entry, axis=1)).astype(jnp.bfloat16)
    return lax.psum_scatter(
        jnp.dot(attended, w_out, preferred_element_type=jnp.float32),
        "ctx",
        scatter_dimension=0,
        tiled=True,
    ).astype(jnp.bfloat16)


MESH = pl.DeviceIdType.MESH
EXP_SCALE = HEAD ** (-0.5) * 1.4426950408889634
GROUP = HEADS // KV_HEADS
OWN = GROUP // 2
CHUNKS = 4
CHUNK_COLS = D // CHUNKS
TILE = CHUNK_COLS // 2


def fused_kernel(
    q_ref, ids_hbm, table_hbm, blocks_hbm, kv_hbm, w_hbm, out_ref,
    ids_ref, table_ref, blocks_ref, kv_ref, w_ref, q_all, bias_ref, q_rows, v_t,
    o_send, s_send, o_keep, s_keep, r1, rs1,
    t1s, ts1s, t1k, ts1k, r2, rs2,
    t2s, ts2s, t2k, ts2k, r3, rs3,
    t3s, ts3s, t3k, ts3k, r4, rs4,
    att, p0, p0s, pr1, p1, p1s, pr2, p2, p2s, pr3, p3, p3s, pr4,
    ids_sem, table_sem, blocks_sem, kv_sem, w_sem,
    ag_send, ag_recv, rs_send, rs_recv, ss_send, ss_recv, pj_send, pj_recv,
):
    me = lax.axis_index("ctx")
    core = me % 2
    y = (me // 2) % 2
    z0 = (me // 4) % 2
    z1 = me // 8
    to_core = me + 1 - 2 * core
    to_y = me + 2 - 4 * y
    to_z0 = me + 4 - 8 * z0
    to_z1 = me + 8 - 16 * z1
    groups = q_all.shape[0]
    rows = q_ref.shape[0]
    keys = kv_ref.shape[1]
    key_blocks = keys // BLOCK
    queries = rows * 2 * groups

    kv_load = pltpu.make_async_copy(kv_hbm, kv_ref, kv_sem)
    w_load = pltpu.make_async_copy(w_hbm, w_ref, w_sem)
    ids_load = pltpu.make_async_copy(ids_hbm, ids_ref, ids_sem)
    table_load = pltpu.make_async_copy(table_hbm, table_ref, table_sem)
    blocks_load = pltpu.make_async_copy(blocks_hbm, blocks_ref, blocks_sem)
    for load in (ids_load, table_load, blocks_load, kv_load, w_load):
        load.start()

    barrier = pltpu.get_barrier_semaphore()
    for other in (to_core, to_y, to_z0, to_z1):
        pl.semaphore_signal(barrier, inc=1, device_id={"ctx": other}, device_id_type=MESH)

    ids_load.wait()
    table_load.wait()
    blocks_load.wait()
    row_at = lax.broadcasted_iota(jnp.int32, (rows, rows), 0)
    lane_at = lax.broadcasted_iota(jnp.int32, (rows, rows), 1)
    ids_wide = jnp.broadcast_to(ids_ref[...].astype(jnp.float32), (rows, rows))
    ids_col = jnp.sum(jnp.where(row_at == lane_at, ids_wide, 0.0), axis=1, keepdims=True)
    lookup_ids = lax.broadcasted_iota(jnp.int32, (rows, table_ref.shape[0]), 1)
    one_hot = jnp.where(ids_col == lookup_ids.astype(jnp.float32), 1.0, 0.0).astype(jnp.bfloat16)
    for g in range(groups):
        cols = slice(g * GROUP * HEAD, (g + 1) * GROUP * HEAD)
        lookup = jnp.dot(one_hot, table_ref[:, cols], preferred_element_type=jnp.float32)
        steered = q_ref[:, cols].astype(jnp.float32) + lookup
        stacked = jnp.concatenate(
            [steered[:, h * HEAD:(h + 1) * HEAD] for h in range(GROUP)], axis=0
        )
        q_all[g, z1, z0, y, core] = stacked.astype(jnp.bfloat16)

    def remote(src, dst, send, recv, other):
        return pltpu.make_async_remote_copy(
            src_ref=src, dst_ref=dst, send_sem=send, recv_sem=recv,
            device_id={"ctx": other}, device_id_type=MESH,
        )

    def gather(step, g):
        if step == 0:
            ref, other = q_all.at[g, z1, z0, y, core], to_z1
        elif step == 1:
            ref, other = q_all.at[g, :, z0, y, core], to_z0
        elif step == 2:
            ref, other = q_all.at[g, :, :, y, core], to_y
        else:
            ref, other = q_all.at[g, :, :, :, core], to_core
        return remote(ref, ref, ag_send.at[step, g], ag_recv.at[step, g], other)

    def pick(mine, bit):
        return mine * bit + (1 - mine) * (1 - bit)

    def order(step, p):
        a = z1 if step >= 1 else 1 - z1
        b = z0 if step >= 2 else 1 - z0
        c = y if step >= 3 else 1 - y
        return 4 * pick(a, p // 4) + 2 * pick(b, (p // 2) % 2) + pick(c, p % 2)

    def merge_copies(step, i):
        if step == 0:
            a, b, other = (o_send.at[i], r1.at[i]), (s_send.at[i], rs1.at[i]), to_core
        elif step == 1:
            a, b, other = (t1s.at[i], r2.at[i]), (ts1s.at[i], rs2.at[i]), to_y
        elif step == 2:
            a, b, other = (t2s.at[i], r3.at[i]), (ts2s.at[i], rs3.at[i]), to_z0
        else:
            a, b, other = (t3s.at[i], r4.at[i]), (ts3s.at[i], rs4.at[i]), to_z1
        return (
            remote(a[0], a[1], rs_send.at[step, i], rs_recv.at[step, i], other),
            remote(b[0], b[1], ss_send.at[step, i], ss_recv.at[step, i], other),
        )

    def start_merge(step, i):
        for copy in merge_copies(step, i):
            copy.start()

    def wait_merge(step, i):
        for copy in merge_copies(step, i):
            copy.wait_recv()

    def merge_stats(sa, sb):
        ma, mb = sa[:OWN], sb[:OWN]
        peak = jnp.maximum(ma, mb)
        wa = jnp.exp2((ma - peak) * EXP_SCALE)
        wb = jnp.exp2((mb - peak) * EXP_SCALE)
        return peak, wa, wb, wa * sa[OWN:] + wb * sb[OWN:]

    def merge(oa, sa, ob, sb, o_dst, s_dst):
        peak, wa, wb, total = merge_stats(sa[...], sb[...])
        s_dst[...] = jnp.concatenate([peak, total], axis=0)
        for h in range(OWN):
            o_dst[h] = (
                oa[h].astype(jnp.float32) * wa[h:h + 1]
                + ob[h].astype(jnp.float32) * wb[h:h + 1]
            ).astype(o_dst.dtype)

    first = me * key_blocks
    block_ids = first + lax.broadcasted_iota(jnp.int32, (key_blocks, blocks_ref.shape[1]), 0)
    lane_block = (lax.broadcasted_iota(jnp.int32, (key_blocks, 2 * queries), 1) % queries) // BLOCK
    bias = jnp.zeros((key_blocks, 2 * queries), jnp.float32)
    for b in range(blocks_ref.shape[0]):
        same = jnp.where(block_ids == blocks_ref[b:b + 1, :], 1.0, 0.0)
        hit = jnp.max(same, axis=1, keepdims=True)
        bias = jnp.where(lane_block == b, (hit - 1.0) * 1e30, bias)
    bias_ref[...] = bias

    pl.semaphore_wait(barrier, 4)

    @pl.loop(0, groups)
    def _(p):
        gather(0, order(0, p)).start()

    def attend(g):
        lanes = pl.ds(pl.multiple_of(g * HEAD, HEAD), HEAD)
        v_t[...] = kv_ref[1, :, lanes].T
        q_wide = q_all[g].reshape(2 * groups, GROUP * rows, HEAD).astype(jnp.float32)
        for h in range(GROUP):
            head_rows = q_wide[:, h * rows:(h + 1) * rows, :].reshape(queries, HEAD)
            q_rows[h // 2, (h % 2) * queries:(h % 2 + 1) * queries] = head_rows.astype(jnp.bfloat16)

        def heads(half, o_dst, s_dst):
            @pl.loop(0, OWN // 2)
            def _(i):
                scores = lax.dot_general(
                    kv_ref[0, :, lanes], q_rows[half * (OWN // 2) + i], (((1,), (1,)), ((), ())),
                    preferred_element_type=jnp.float32,
                )
                scores = scores.reshape(key_blocks, BLOCK, 2 * queries) + bias_ref[...][:, None, :]
                scores = scores.reshape(keys, 2 * queries)
                peak = jnp.max(scores, axis=0, keepdims=True)
                weights = jnp.exp2((scores - peak) * EXP_SCALE)
                total = jnp.sum(weights, axis=0, keepdims=True)
                part = jnp.dot(v_t[...], weights.astype(jnp.bfloat16), preferred_element_type=jnp.float32)
                for h in range(2):
                    lane = slice(h * queries, (h + 1) * queries)
                    o_dst[g, 2 * i + h] = part[:, lane].astype(o_dst.dtype)
                    s_dst[g, pl.ds(2 * i + h, 1), :] = peak[:, lane]
                    s_dst[g, pl.ds(OWN + 2 * i + h, 1), :] = total[:, lane]

        heads(1 - core, o_send, s_send)
        start_merge(0, g)
        heads(core, o_keep, s_keep)

    def at(cond, fn):
        pl.when(cond)(fn)

    @pl.loop(0, groups + 9)
    def _(t):
        for step in range(3):
            def advance(step=step):
                g = order(step + 1, t - 2 * step)
                gather(step, g).wait_recv()
                gather(step + 1, g).start()
            at((t >= 2 * step) & (t < groups + 2 * step), advance)

        def merge_core():
            p = t - 7
            g = order(3, p)
            j = g // 2
            wait_merge(0, g)
            parts = (o_keep.at[g], s_keep.at[g], r1.at[g], rs1.at[g])

            def send():
                merge(*parts, t1s.at[j], ts1s.at[j])
                start_merge(1, j)
            at(p % 2 == 0, send)
            at(p % 2 == 1, lambda: merge(*parts, t1k.at[j], ts1k.at[j]))
        at((t >= 7) & (t < groups + 7), merge_core)

        def merge_y():
            p = t - 8
            j = order(3, p) // 2
            k = j // 2
            wait_merge(1, j)
            parts = (t1k.at[j], ts1k.at[j], r2.at[j], rs2.at[j])

            def send():
                merge(*parts, t2s.at[k], ts2s.at[k])
                start_merge(2, k)
            at(p % 4 == 1, send)
            at(p % 4 == 3, lambda: merge(*parts, t2k.at[k], ts2k.at[k]))
        at((t >= 9) & (t < groups + 8) & (t % 2 == 1), merge_y)

        def merge_z0():
            p = t - 9
            k = order(3, p) // 4
            wait_merge(2, k)
            parts = (t2k.at[k], ts2k.at[k], r3.at[k], rs3.at[k])

            def send():
                merge(*parts, t3s.at[0], ts3s.at[0])
                start_merge(3, 0)
            at(p == 3, send)
            at(p == 7, lambda: merge(*parts, t3k.at[0], ts3k.at[0]))
        at((t == 12) | (t == 16), merge_z0)

        def attention():
            g = order(3, t - 6)
            gather(3, g).wait_recv()
            at(t == 6, kv_load.wait)
            attend(g)
        at((t >= 6) & (t < groups + 6), attention)

    w_load.wait()
    wait_merge(3, 0)
    peak, wa, wb, total = merge_stats(ts3k[0], rs4[0])
    inverse = 1.0 / total
    wa, wb = wa * inverse, wb * inverse
    for h in range(OWN):
        done = t3k[0, h] * wa[h:h + 1] + r4[0, h].astype(jnp.float32) * wb[h:h + 1]
        att[:, h * HEAD:(h + 1) * HEAD] = done.T.astype(jnp.bfloat16)

    def project_copy(step, c):
        swap = c % 2 == 1
        if step == 0:
            src, dst, other = p0s.at[c], pr1.at[c], to_core
        elif step == 1:
            src, dst, other = p1s.at[c], pr2.at[c], to_z0 if swap else to_y
        elif step == 2:
            src, dst, other = p2s.at[c], pr3.at[c], to_y if swap else to_z0
        else:
            src, dst, other = p3s.at[c], pr4.at[c], to_z1
        return remote(src, dst, pj_send.at[step, c], pj_recv.at[step, c], other)

    def stage(step, c):
        swap = c % 2 == 1
        low = jnp.bfloat16
        if step > 0:
            project_copy(step - 1, c).wait_recv()
        if step == 0:
            halves = []
            for i in range(2):
                base = c * CHUNK_COLS + i * TILE
                part = jnp.dot(att[...], w_ref[:, base:base + TILE], preferred_element_type=jnp.float32)
                halves.append(part.reshape(2 * groups, rows, TILE))
            both = jnp.concatenate(halves, axis=1)
            p0[c] = both.reshape(2, 2, 2, 2, 2 * rows, TILE)
            p0s[c] = p0[c, :, :, :, 1 - core].astype(low)
        elif step == 1:
            p1[c] = p0[c, :, :, :, core] + pr1[c].astype(jnp.float32)
            p1s[c] = (p1[c, :, 1 - z0] if swap else p1[c, :, :, 1 - y]).astype(low)
        elif step == 2:
            p2[c] = (p1[c, :, z0] if swap else p1[c, :, :, y]) + pr2[c].astype(jnp.float32)
            p2s[c] = (p2[c, :, 1 - y] if swap else p2[c, :, 1 - z0]).astype(low)
        elif step == 3:
            p3[c] = (p2[c, :, y] if swap else p2[c, :, z0]) + pr3[c].astype(jnp.float32)
            p3s[c] = p3[c, 1 - z1].astype(low)
        else:
            done = p3[c, z1] + pr4[c].astype(jnp.float32)
            for i in range(2):
                base = c * CHUNK_COLS + i * TILE
                out_ref[:, base:base + TILE] = done[i * rows:(i + 1) * rows].astype(low)
        if step < 4:
            project_copy(step, c).start()

    for step in range(5):
        for c in range(CHUNKS):
            stage(step, c)

    @pl.loop(0, groups)
    def _(g):
        for step in range(4):
            gather(step, g).wait_send()

    for step in range(4):
        for i in range(max(groups >> step, 1)):
            for copy in merge_copies(step, i):
                copy.wait_send()
        for c in range(CHUNKS):
            project_copy(step, c).wait_send()


def per_device_fused(queries, steer_ids, steer_table, kv, blocks, w_out):
    rows = queries.shape[0]
    keys = kv.shape[1]
    groups = KV_HEADS
    total_q = 2 * groups * rows
    bf, f32 = jnp.bfloat16, jnp.float32
    piece = (OWN, HEAD, total_q)
    stat = (2 * OWN, total_q)
    tile = (2 * rows, TILE)
    scratch = [
        pltpu.VMEM((1, rows), jnp.int32),
        pltpu.VMEM(steer_table.shape, bf),
        pltpu.VMEM(blocks.shape, jnp.int32),
        pltpu.VMEM(kv.shape, bf),
        pltpu.VMEM(w_out.shape, bf),
        pltpu.VMEM((groups, 2, 2, 2, 2, GROUP * rows, HEAD), bf),
        pltpu.VMEM((keys // BLOCK, 2 * total_q), f32),
        pltpu.VMEM((GROUP // 2, 2 * total_q, HEAD), bf),
        pltpu.VMEM((HEAD, keys), bf),
    ]
    for count in (groups, groups // 2, groups // 4, groups // 8):
        for kind in (bf, f32, bf):
            scratch += [pltpu.VMEM((count,) + piece, kind), pltpu.VMEM((count,) + stat, f32)]
    scratch += [pltpu.VMEM((total_q, OWN * HEAD), bf), pltpu.VMEM((CHUNKS, 2, 2, 2, 2) + tile, f32)]
    for lead in ((2, 2, 2), (2, 2), (2,)):
        many = (CHUNKS,) + lead + tile
        scratch += [pltpu.VMEM(many, bf), pltpu.VMEM(many, bf), pltpu.VMEM(many, f32)]
    scratch += [pltpu.VMEM((CHUNKS,) + tile, bf), pltpu.VMEM((CHUNKS,) + tile, bf)]
    dma = pltpu.SemaphoreType.DMA
    scratch += [dma(())] * 5 + [dma((4, groups))] * 6 + [dma((4, CHUNKS))] * 2
    vmem = pl.BlockSpec(memory_space=pltpu.VMEM)
    hbm = pl.BlockSpec(memory_space=pl.ANY)
    return pl.pallas_call(
        fused_kernel,
        out_shape=jax.ShapeDtypeStruct(queries.shape, bf),
        in_specs=[vmem, hbm, hbm, hbm, hbm, hbm],
        out_specs=vmem,
        scratch_shapes=scratch,
        compiler_params=pltpu.CompilerParams(
            collective_id=0, has_side_effects=True, vmem_limit_bytes=48 * 1024 * 1024
        ),
    )(queries, steer_ids[None, :], steer_table, blocks, kv, w_out)


def solution(mesh):
    fits = mesh.shape["ctx"] == 2 * KV_HEADS
    return jax.shard_map(
        per_device_fused if fits else per_device,
        mesh=mesh,
        in_specs=(
            P(("parts", "ctx"), None),
            P(("parts", "ctx")),
            P(),
            P(None, ("parts", "ctx"), None),
            P("parts", None),
            P("ctx", None),
        ),
        out_specs=P(("parts", "ctx"), None),
        check_vma=False,
    )
```
